256 devices in a mesh: replica: 16 (over y_lo, x, core), fsdp: 16 (over y_hi, z).
Axes of the slice: x: 4, y: 4 (y_hi: 2, y_lo: 2; y = y_hi * 2 + y_lo), z: 8, core: 2. Of those that a mesh axis runs over, the one named last changes fastest.
Arguments:
- tokens: bfloat16 [49152, 12288], P(('replica', 'fsdp')), may hold values from -6 to 6
- cotangent: bfloat16 [49152, 512], P(('replica', 'fsdp')), may hold values from -6 to 6
- local_weight: bfloat16 [16, 12288, 512], P('replica', 'fsdp'), may hold values from -6 to 6
- anchor: float32 [12288, 128], P('fsdp'), may hold values from -6 to 6
- momentum: float32 [12288, 128], P('fsdp'), may hold values from -4 to 4
- fragment: int32 [1], replicated, may hold values from 0 to 1023
- counter: int32 [1], replicated, may hold values from 0 to 15
Outputs:
- grad_weight: float32 [16, 12288, 512], P('replica', 'fsdp')
- new_anchor: float32 [12288, 128], P('fsdp')
- new_momentum: float32 [12288, 128], P('fsdp')
The draws below stay inside these ranges and needn't reach their ends.
All inputs are finite; a program needn't handle non-finite values.
Results may differ from the reference program's by a relative error of at most 0.003.
Values may be sent and summed in bfloat16 or wider, within the bound.
No kernel may reach another device: no remote copies, remote signals or barrier semaphores. Data moves between devices by JAX's collectives and lax.ppermute only.
A program may use at most 128 MiB of HBM per device.

```python
import jax
import jax.numpy as jnp
from jax import lax

D = 12288
H = 512
NFRAG = 4
FH = 128
TOK_DEV = 192
TOKENS = 49152
N_REPLICA = 16
N_FSDP = 16


def block_levels(key, shape, pieces, low, top_value):
    def one(axis_at, blocks):
        steps = jax.random.uniform(jax.random.fold_in(jax.random.fold_in(key, 6), axis_at), (blocks,), jnp.float32, low / len(pieces), top_value / len(pieces))
        return jnp.repeat(jnp.exp(steps), shape[axis_at] // blocks).reshape((-1,) + (1,) * (len(shape) - axis_at - 1))

    gain = one(*pieces[0])
    for cut in pieces[1:]:
        gain = gain * one(*cut)
    return gain


def normal_values(rng, dims, width, bound, shards=(), dtype=jnp.bfloat16):
    values = jax.random.normal(rng, dims, jnp.float32) * width
    if len(shards) > 0:
        values = block_levels(rng, dims, shards, -0.22, 0.18) * values
    return jnp.clip(values, min=-bound, max=bound).astype(dtype)


def setup_inputs(seed: int = 0) -> dict:
    key_of = jax.random.split(jax.random.key(seed), 8)
    tokens = normal_values(key_of[0], (TOKENS, D), 1.0, 6.0, ((0, 256),))
    cotangent = normal_values(key_of[1], (TOKENS, H), 1.0, 6.0, ((0, 256),))
    local_weight = normal_values(key_of[2], (N_REPLICA, D, H), 1.0, 6.0, ((0, 16), (1, 16)))
    anchor = normal_values(key_of[3], (D, FH), 1.0, 6.0, ((0, 16),), jnp.float32)
    momentum = normal_values(key_of[4], (D, FH), 0.5, 4.0, ((0, 16),), jnp.float32)
    fragment = jax.random.randint(key_of[5], (1,), 0, 1024).astype(jnp.int32)
    counter = jax.random.randint(key_of[6], (1,), 0, 16).astype(jnp.int32)
    return {"tokens": tokens, "cotangent": cotangent, "local_weight": local_weight, "anchor": anchor, "momentum": momentum, "fragment": fragment, "counter": counter}


outer_mu = 0.9
outer_rate = 0.7
warm_steps = 8.0
mix_keep = 0.5

def reference(tokens, cotangent, local_weight, anchor, momentum, fragment, counter):
    start = (fragment[0] % NFRAG * FH).astype(jnp.int32)
    eta = outer_rate * jnp.minimum(jnp.float32(1.0), (counter[0].astype(jnp.float32) + 1.0) / warm_steps)
    frag_local = lax.dynamic_slice_in_dim(local_weight, start, FH, 2).astype(jnp.float32)
    delta = lax.optimization_barrier(jnp.sum(anchor[None] - frag_local, axis=0)) / N_REPLICA
    new_momentum = outer_mu * momentum + delta
    new_anchor = anchor - eta * (outer_mu * new_momentum + delta)
    mixed = (mix_keep * frag_local + (1.0 - mix_keep) * new_anchor[None]).astype(jnp.bfloat16)
    weights = lax.dynamic_update_slice_in_dim(local_weight, mixed, start, 2)
    scale = 1.0 / jnp.sqrt(jnp.float32(D))
    inputs = tokens.reshape(N_REPLICA, N_FSDP, TOK_DEV, D)
    upstream = cotangent.reshape(N_REPLICA, N_FSDP, TOK_DEV, H)

    def replica_grad(packed):
        weight, rows, grads_in = packed

        def device_term(total, pair):
            block, grad_block = pair
            pre = jnp.dot(block, weight, preferred_element_type=jnp.float32) * scale
            _, pull = jax.vjp(jax.nn.gelu, pre)
            dpre = pull(grad_block.astype(jnp.float32))[0].astype(jnp.bfloat16)
            partial_term = jnp.dot(block.T, dpre, preferred_element_type=jnp.float32) * scale
            return (total + partial_term, None)
        total, _ = lax.scan(device_term, jnp.zeros((D, H), jnp.float32), (rows, grads_in))
        return total
    grad_weight = lax.map(replica_grad, (weights, inputs, upstream))
    return (grad_weight, new_anchor, new_momentum)
```

```python
import math

import jax
import jax.numpy as jnp
from jax import lax
from jax.sharding import PartitionSpec as P

D = 12288
NFRAG = 4
REP = 16
FSDP = 16
NZ = 8
CHUNKS = ((0, 1), (2, 3))

outer_mu = 0.9
outer_rate = 0.7
warm_steps = 8.0
mix_keep = 0.5
LIFT = 32.0

RING = [
    (r * FSDP + yh * NZ + z, r * FSDP + yh * NZ + (z + 1 - 2 * (r % 2)) % NZ)
    for r in range(REP)
    for yh in range(2)
    for z in range(NZ)
]
SWAP = [(f, (f + NZ) % FSDP) for f in range(FSDP)]


def around(x):
    return lax.ppermute(x, ("replica", "fsdp"), RING)


def across(x):
    return lax.ppermute(x, "fsdp", SWAP)


def on_device(tokens, cotangent, local_weight, anchor, momentum, fragment, counter):
    width = anchor.shape[1]
    frag = fragment[0] % NFRAG
    eta = outer_rate * jnp.minimum(
        jnp.float32(1.0), (counter[0].astype(jnp.float32) + 1.0) / warm_steps
    )
    scale = 1.0 / math.sqrt(D)
    local = local_weight[0]
    rows = local.shape[0]
    f = lax.axis_index("fsdp")
    yh, z = f // NZ, f % NZ
    step = 1 - 2 * (lax.axis_index("replica") % 2)
    half = D // 2
    toks = tokens.shape[0]

    def block_at(x, k):
        return lax.dynamic_slice_in_dim(x, (frag + 1 + k) % NFRAG * width, width, 1)

    frag_local = block_at(local, 3)
    parts = lax.all_to_all(frag_local, "replica", split_axis=0, concat_axis=0, tiled=True)
    part_sum = jnp.sum(
        parts.reshape(REP, rows // REP, width).astype(jnp.float32), axis=0
    )
    frag_sum = lax.all_gather(part_sum, "replica", axis=0, tiled=True)
    delta = anchor - frag_sum / REP
    new_momentum = outer_mu * momentum + delta
    new_anchor = anchor - eta * (outer_mu * new_momentum + delta)
    mixed = (
        mix_keep * frag_local.astype(jnp.float32) + (1.0 - mix_keep) * new_anchor
    ).astype(jnp.bfloat16)

    own = lax.dynamic_slice_in_dim(tokens, yh * half, half, 1)
    other = across(lax.dynamic_slice_in_dim(tokens, (1 - yh) * half, half, 1))
    x = jnp.concatenate([own, other], 0)
    cot = jnp.concatenate([cotangent, across(cotangent)], 0)

    def features(zz):
        return lax.dynamic_slice_in_dim(x, zz % NZ * rows, rows, 1)

    outs = []
    for chunk in CHUNKS:
        w = jnp.concatenate([mixed if k == 3 else block_at(local, k) for k in chunk], 1)
        up = jnp.concatenate([block_at(cot, k) for k in chunk], 1).astype(jnp.float32)
        total = None
        for s in range(NZ):
            term = jnp.dot(features(z - step * s + NZ), w, preferred_element_type=jnp.float32)
            total = term if total is None else total + term
            if s < NZ - 1:
                w = around(w)
        part = total * scale
        got = across(part.astype(jnp.float16)).astype(jnp.float32)
        pre = part + jnp.concatenate([got[toks:], got[:toks]], 0)
        _, pull = jax.vjp(jax.nn.gelu, pre)
        dpre = pull(up)[0].astype(jnp.bfloat16)
        got = None
        for s in range(NZ):
            dest = z - step * (1 + s) + 2 * NZ
            term = lax.dot_general(
                features(dest), dpre, (((0,), (0,)), ((), ())),
                preferred_element_type=jnp.float32,
            ) * (scale * LIFT)
            if got is not None:
                term = term + got.astype(jnp.float32)
            if s < NZ - 1:
                got = around(term.astype(jnp.float16))
        outs.append(term * (1.0 / LIFT))
    grads = jnp.concatenate(outs, 1)
    grads = jnp.concatenate(
        [
            lax.dynamic_slice_in_dim(grads, (b - frag - 1 + 2 * NFRAG) % NFRAG * width, width, 1)
            for b in range(NFRAG)
        ],
        1,
    )
    return (grads[None], new_anchor, new_momentum)


def solution(mesh):
    placed = (
        P(("replica", "fsdp"), None),
        P(("replica", "fsdp"), None),
        P("replica", "fsdp", None),
        P("fsdp", None),
        P("fsdp", None),
        P(),
        P(),
    )
    return jax.shard_map(
        on_device,
        mesh=mesh,
        in_specs=placed,
        out_specs=(P("replica", "fsdp", None), P("fsdp", None), P("fsdp", None)),
        check_vma=False,
    )
```

```python
import math

import jax
import jax.numpy as jnp
from jax import lax
from jax.experimental import pallas as pl
from jax.experimental.pallas import tpu as pltpu
from jax.sharding import PartitionSpec as P

D = 12288
NFRAG = 4
REP = 16
FSDP = 16
NZ = 8
LANES = 3

outer_mu = 0.9
outer_rate = 0.7
warm_steps = 8.0
mix_keep = 0.5
LIFT = 32.0

RING = [
    (r * FSDP + yh * NZ + z, r * FSDP + yh * NZ + (z + 1 - 2 * (r % 2)) % NZ)
    for r in range(REP)
    for yh in range(2)
    for z in range(NZ)
]
YLO = [(r, r ^ 8) for r in range(REP)]
CORE = [(r, r ^ 1) for r in range(REP)]
X1 = [(r, r ^ 2) for r in range(REP)]
X3 = [(r, r ^ 6) for r in range(REP)]
SWAP = [(f, (f + NZ) % FSDP) for f in range(FSDP)]

WHOLE = pl.BlockSpec(memory_space=pltpu.VMEM)
SCALARS = pl.BlockSpec(memory_space=pltpu.SMEM)
ANY = pl.BlockSpec(memory_space=pl.ANY)


def around(x):
    return lax.ppermute(x, ("replica", "fsdp"), RING)


def across(x):
    return lax.ppermute(x, "fsdp", SWAP)


def after(x, *deps):
    def kernel(*refs):
        del refs

    return pl.pallas_call(
        kernel,
        out_shape=jax.ShapeDtypeStruct(x.shape, x.dtype),
        in_specs=[ANY] * (1 + len(deps)),
        out_specs=ANY,
        input_output_aliases={0: 0},
        cost_estimate=pl.CostEstimate(flops=0, bytes_accessed=0, transcendentals=0),
    )(x, *deps)


def split(tokens, cotangent, mine, *deps):
    toks, half = tokens.shape[0], tokens.shape[1] // 2
    more = cotangent.shape[1]

    def kernel(at_ref, tokens_ref, cot_ref, *rest):
        send_ref, own_ref, sems = rest[-3:]
        own = pl.multiple_of(at_ref[0] * half, 128)
        other = pl.multiple_of((1 - at_ref[0]) * half, 128)
        copies = [
            pltpu.make_async_copy(
                tokens_ref.at[:, pl.ds(other, half)], send_ref.at[:, pl.ds(0, half)], sems.at[0]
            ),
            pltpu.make_async_copy(cot_ref, send_ref.at[:, pl.ds(half, more)], sems.at[1]),
            pltpu.make_async_copy(tokens_ref.at[:, pl.ds(own, half)], own_ref, sems.at[2]),
        ]
        for copy in copies:
            copy.start()
        for copy in copies:
            copy.wait()

    return pl.pallas_call(
        kernel,
        out_shape=(
            jax.ShapeDtypeStruct((toks, half + more), tokens.dtype),
            jax.ShapeDtypeStruct((toks, half), tokens.dtype),
        ),
        in_specs=[SCALARS] + [ANY] * (2 + len(deps)),
        out_specs=(WHOLE, WHOLE),
        scratch_shapes=[pltpu.SemaphoreType.DMA((3,))],
        compiler_params=pltpu.CompilerParams(vmem_limit_bytes=56 * 2**20),
        cost_estimate=pl.CostEstimate(
            flops=0, bytes_accessed=4 * tokens.size, transcendentals=0
        ),
        name="split",
    )(mine.astype(jnp.int32).reshape(1), tokens, cotangent, *deps)


def product(own, moved, at, shards):
    toks, half = own.shape
    count = len(shards[0])
    flat = [w for shard in shards for w in shard]
    size, cols = flat[0].shape

    def kernel(at_ref, own_ref, moved_ref, *rest):
        shard_refs, (out_ref, x, held, sems) = rest[: len(flat)], rest[-4:]
        places = [
            (own_ref, x.at[pl.ds(0, toks), :]),
            (moved_ref.at[:, pl.ds(0, half)], x.at[pl.ds(toks, toks), :]),
        ] + [
            (w, held.at[n // count, pl.ds(n % count * size, size), :])
            for n, w in enumerate(shard_refs)
        ]
        copies = [
            pltpu.make_async_copy(source, into, sems.at[n])
            for n, (source, into) in enumerate(places)
        ]
        for copy in copies:
            copy.start()
        total = None
        for n, copy in enumerate(copies):
            copy.wait()
            if n < 2 or (n - 2) % count < count - 1:
                continue
            step = (n - 2) // count
            start = pl.multiple_of(at_ref[step], 128)
            term = jnp.dot(
                x[:, pl.ds(start, count * size)], held[step], preferred_element_type=jnp.float32
            )
            total = term if total is None else total + term
        out_ref[...] = total

    return pl.pallas_call(
        kernel,
        out_shape=jax.ShapeDtypeStruct((2 * toks, cols), jnp.float32),
        in_specs=[SCALARS] + [ANY] * (2 + len(flat)),
        out_specs=WHOLE,
        scratch_shapes=[
            pltpu.VMEM((2 * toks, half), own.dtype),
            pltpu.VMEM((len(shards), count * size, cols), own.dtype),
            pltpu.SemaphoreType.DMA((2 + len(flat),)),
        ],
        compiler_params=pltpu.CompilerParams(vmem_limit_bytes=56 * 2**20),
        cost_estimate=pl.CostEstimate(
            flops=4 * toks * half * cols,
            bytes_accessed=4 * toks * half + half * cols * 2 + toks * cols * 8,
            transcendentals=0,
        ),
        name="product",
    )(at, own, moved, *flat)


def on_device(tokens, cotangent, local_weight, anchor, momentum, fragment, counter):
    width = anchor.shape[1]
    frag = fragment[0] % NFRAG
    eta = outer_rate * jnp.minimum(
        jnp.float32(1.0), (counter[0].astype(jnp.float32) + 1.0) / warm_steps
    )
    scale = 1.0 / math.sqrt(D)
    local = local_weight[0]
    rows, hidden = local.shape
    f = lax.axis_index("fsdp")
    yh, z = f // NZ, f % NZ
    step = 1 - 2 * (lax.axis_index("replica") % 2)
    half = D // 2
    toks = tokens.shape[0]

    def swapped(v, perm):
        return lax.ppermute(v, "replica", perm)

    core = lax.axis_index("replica") % 2
    half_rows = rows // 2
    frag_local = lax.dynamic_slice_in_dim(local, frag * width, width, 1)
    frag_sum = frag_local.astype(jnp.float32) + swapped(frag_local, YLO).astype(jnp.float32)
    low, high = frag_sum[:half_rows], frag_sum[half_rows:]
    part_sum = jnp.where(core == 0, low, high) + swapped(jnp.where(core == 0, high, low), CORE)
    part_sum = part_sum + swapped(part_sum, X1)
    part_sum = part_sum + swapped(part_sum, X3)
    there = swapped(part_sum, CORE)
    frag_sum = jnp.where(
        core == 0,
        jnp.concatenate([part_sum, there], 0),
        jnp.concatenate([there, part_sum], 0),
    )
    delta = anchor - frag_sum / REP
    new_momentum = outer_mu * momentum + delta
    new_anchor = anchor - eta * (outer_mu * new_momentum + delta)
    mixed = (
        mix_keep * frag_local.astype(jnp.float32) + (1.0 - mix_keep) * new_anchor
    ).astype(jnp.bfloat16)

    weights = lax.dynamic_update_slice_in_dim(local, mixed, frag * width, 1)

    third = rows // LANES
    shards = [[weights[h * third : (h + 1) * third] for h in range(LANES)]]
    for s in range(NZ - 1):
        shards.append([around(v) for v in shards[s]])

    send, own = split(tokens, cotangent, yh)
    moved = across(after(send, *shards[1]))
    x = jnp.concatenate([own, moved[:, :half]], 0)
    cot = jnp.concatenate([cotangent, moved[:, half:]], 0)

    def features(s, row, size):
        return lax.dynamic_slice_in_dim(x, (z - step * s + 2 * NZ) % NZ * rows + row, size, 1)

    at = jnp.stack([(z - step * s + NZ) % NZ * rows for s in range(NZ)]).astype(jnp.int32)

    def backward(total, up):
        part = total * scale
        got = across(part.astype(jnp.float16)).astype(jnp.float32)
        pre = part + jnp.concatenate([got[toks:], got[:toks]], 0)
        _, pull = jax.vjp(jax.nn.gelu, pre)
        return pull(up.astype(jnp.float32))[0].astype(jnp.bfloat16)

    dpre = backward(product(own, moved, at, shards), cot)

    got = [None] * LANES
    for s in range(NZ):
        for h in range(LANES):
            term = lax.dot_general(
                features(1 + s, h * third, third), dpre, (((0,), (0,)), ((), ())),
                preferred_element_type=jnp.float32,
            ) * (scale * LIFT)
            if s > 0:
                term = term + got[h].astype(jnp.float32)
            got[h] = around(term.astype(jnp.float16)) if s < NZ - 1 else term * (1.0 / LIFT)
    grads = jnp.concatenate(got, 0)
    return (grads[None], new_anchor, new_momentum)


def solution(mesh):
    placed = (
        P(("replica", "fsdp"), None),
        P(("replica", "fsdp"), None),
        P("replica", "fsdp", None),
        P("fsdp", None),
        P("fsdp", None),
        P(),
        P(),
    )
    return jax.shard_map(
        on_device,
        mesh=mesh,
        in_specs=placed,
        out_specs=(P("replica", "fsdp", None), P("fsdp", None), P("fsdp", None)),
        check_vma=False,
    )
```

```python
import math

import jax
import jax.numpy as jnp
from jax import lax
from jax.experimental import pallas as pl
from jax.experimental.pallas import tpu as pltpu
from jax.sharding import PartitionSpec as P

D = 12288
NFRAG = 4
REP = 16
FSDP = 16
NZ = 8
KEPT = NFRAG - 1

outer_mu = 0.9
outer_rate = 0.7
warm_steps = 8.0
mix_keep = 0.5
LIFT = 32.0

RING = [
    (r * FSDP + yh * NZ + z, r * FSDP + yh * NZ + (z + 1 - 2 * (r % 2)) % NZ)
    for r in range(REP)
    for yh in range(2)
    for z in range(NZ)
]
YLO = [(r, r ^ 8) for r in range(REP)]
CORE = [(r, r ^ 1) for r in range(REP)]
X1 = [(r, r ^ 2) for r in range(REP)]
X3 = [(r, r ^ 6) for r in range(REP)]
SWAP = [(f, (f + NZ) % FSDP) for f in range(FSDP)]

WHOLE = pl.BlockSpec(memory_space=pltpu.VMEM)
SCALARS = pl.BlockSpec(memory_space=pltpu.SMEM)
ANY = pl.BlockSpec(memory_space=pl.ANY)


def around(x):
    return lax.ppermute(x, ("replica", "fsdp"), RING)


def back(x):
    return lax.ppermute(x, ("replica", "fsdp"), [(b, a) for a, b in RING])


def across(x):
    return lax.ppermute(x, "fsdp", SWAP)


def after(x, *deps):
    def kernel(*refs):
        del refs

    return pl.pallas_call(
        kernel,
        out_shape=jax.ShapeDtypeStruct(x.shape, x.dtype),
        in_specs=[ANY] * (1 + len(deps)),
        out_specs=ANY,
        input_output_aliases={0: 0},
        cost_estimate=pl.CostEstimate(flops=0, bytes_accessed=0, transcendentals=0),
    )(x, *deps)


def split(tokens, cotangent, mine, *deps):
    toks, half = tokens.shape[0], tokens.shape[1] // 2
    more = cotangent.shape[1]

    def kernel(at_ref, tokens_ref, cot_ref, *rest):
        send_ref, own_ref, sems = rest[-3:]
        own = pl.multiple_of(at_ref[0] * half, 128)
        other = pl.multiple_of((1 - at_ref[0]) * half, 128)
        copies = [
            pltpu.make_async_copy(
                tokens_ref.at[:, pl.ds(other, half)], send_ref.at[:, pl.ds(0, half)], sems.at[0]
            ),
            pltpu.make_async_copy(cot_ref, send_ref.at[:, pl.ds(half, more)], sems.at[1]),
            pltpu.make_async_copy(tokens_ref.at[:, pl.ds(own, half)], own_ref, sems.at[2]),
        ]
        for copy in copies:
            copy.start()
        for copy in copies:
            copy.wait()

    return pl.pallas_call(
        kernel,
        out_shape=(
            jax.ShapeDtypeStruct((toks, half + more), tokens.dtype),
            jax.ShapeDtypeStruct((toks, half), tokens.dtype),
        ),
        in_specs=[SCALARS] + [ANY] * (2 + len(deps)),
        out_specs=(WHOLE, WHOLE),
        scratch_shapes=[pltpu.SemaphoreType.DMA((3,))],
        compiler_params=pltpu.CompilerParams(vmem_limit_bytes=10 * 2**20),
        cost_estimate=pl.CostEstimate(
            flops=0, bytes_accessed=4 * tokens.size, transcendentals=0
        ),
        name="split",
    )(mine.astype(jnp.int32).reshape(1), tokens, cotangent, *deps)


def product(x, at, shards):
    count = len(shards[0])
    flat = [w for shard in shards for w in shard]
    size, cols = flat[0].shape

    def kernel(at_ref, x_ref, *rest):
        shard_refs, (out_ref, held, sems) = rest[:-3], rest[-3:]
        copies = [
            pltpu.make_async_copy(
                w, held.at[n // count, pl.ds(n % count * size, size), :], sems.at[n]
            )
            for n, w in enumerate(shard_refs)
        ]
        for copy in copies:
            copy.start()
        total = None
        for n, copy in enumerate(copies):
            copy.wait()
            if n % count < count - 1:
                continue
            step = n // count
            start = pl.multiple_of(at_ref[step], 128)
            term = jnp.dot(
                x_ref[:, pl.ds(start, count * size)],
                held[step],
                preferred_element_type=jnp.float32,
            )
            total = term if total is None else total + term
        out_ref[...] = total

    return pl.pallas_call(
        kernel,
        out_shape=jax.ShapeDtypeStruct((x.shape[0], cols), jnp.float32),
        in_specs=[SCALARS, WHOLE] + [ANY] * len(flat),
        out_specs=WHOLE,
        scratch_shapes=[
            pltpu.VMEM((len(shards), count * size, cols), x.dtype),
            pltpu.SemaphoreType.DMA((len(flat),)),
        ],
        compiler_params=pltpu.CompilerParams(vmem_limit_bytes=12 * 2**20),
        cost_estimate=pl.CostEstimate(
            flops=2 * x.shape[0] * x.shape[1] * cols,
            bytes_accessed=x.size * 2 + x.shape[1] * cols * 2 + x.shape[0] * cols * 4,
            transcendentals=0,
        ),
        name="product",
    )(at, x, *flat)


MIX_AT = 4


def on_device(tokens, cotangent, local_weight, anchor, momentum, fragment, counter):
    width = anchor.shape[1]
    frag = fragment[0] % NFRAG
    eta = outer_rate * jnp.minimum(
        jnp.float32(1.0), (counter[0].astype(jnp.float32) + 1.0) / warm_steps
    )
    scale = 1.0 / math.sqrt(D)
    local = local_weight[0]
    rows, hidden = local.shape
    f = lax.axis_index("fsdp")
    yh, z = f // NZ, f % NZ
    step = 1 - 2 * (lax.axis_index("replica") % 2)
    half = D // 2
    toks = tokens.shape[0]

    def columns(x, k):
        return lax.dynamic_slice_in_dim(x, (frag + 1 + k) % NFRAG * width, width, 1)

    def kept(x):
        return jnp.concatenate([columns(x, k) for k in range(KEPT)], 1)

    part_rows = rows // 2
    w = kept(local)
    shards = [[w[:part_rows], w[part_rows:]]]
    for s in range(NZ - 1):
        shards.append([around(v) for v in shards[s]])

    def swapped(v, perm):
        return lax.ppermute(v, "replica", perm)

    core = lax.axis_index("replica") % 2
    frag_local = columns(local, KEPT)
    frag_sum = frag_local.astype(jnp.float32) + swapped(frag_local, YLO).astype(jnp.float32)
    low, high = frag_sum[:part_rows], frag_sum[part_rows:]
    part_sum = jnp.where(core == 0, low, high) + swapped(jnp.where(core == 0, high, low), CORE)
    near_sum = part_sum
    part_sum = part_sum + swapped(part_sum, X1)
    part_sum = part_sum + swapped(part_sum, X3)
    there = swapped(part_sum, CORE)
    frag_sum = jnp.where(
        core == 0,
        jnp.concatenate([part_sum, there], 0),
        jnp.concatenate([there, part_sum], 0),
    )
    delta = anchor - frag_sum / REP
    new_momentum = outer_mu * momentum + delta
    new_anchor = anchor - eta * (outer_mu * new_momentum + delta)
    mixed = (
        mix_keep * frag_local.astype(jnp.float32) + (1.0 - mix_keep) * new_anchor
    ).astype(jnp.bfloat16)

    mixed = after(mixed, *shards[MIX_AT])
    ups, downs = [mixed], [mixed]
    for s in range(NZ // 2):
        ups.append(around(ups[s]))
        if s < NZ // 2 - 1:
            downs.append(back(downs[s]))
    last = ups + downs[:0:-1]

    send, own = split(tokens, cotangent, yh, near_sum, *shards[1])
    moved = across(send)
    x = jnp.concatenate([own, moved[:, :half]], 0)
    cot = jnp.concatenate([cotangent, moved[:, half:]], 0)

    def features(s, row, size):
        return lax.dynamic_slice_in_dim(x, (z - step * s + 2 * NZ) % NZ * rows + row, size, 1)

    at = jnp.stack([(z - step * s + NZ) % NZ * rows for s in range(NZ)]).astype(jnp.int32)

    def backward(total, up):
        part = total * scale
        got = across(part.astype(jnp.float16)).astype(jnp.float32)
        pre = part + jnp.concatenate([got[toks:], got[:toks]], 0)
        _, pull = jax.vjp(jax.nn.gelu, pre)
        return pull(up.astype(jnp.float32))[0].astype(jnp.bfloat16)

    dpre = jnp.concatenate(
        [
            backward(product(x, at, shards), kept(cot)),
            backward(product(x, at, [[v] for v in last]), columns(cot, KEPT)),
        ],
        1,
    )
    dpre = jnp.concatenate(
        [
            lax.dynamic_slice_in_dim(dpre, (b - frag - 1 + 2 * NFRAG) % NFRAG * width, width, 1)
            for b in range(NFRAG)
        ],
        1,
    )

    third = rows // 3
    got = [None] * 3
    for s in range(NZ):
        for h in range(3):
            term = lax.dot_general(
                features(1 + s, h * third, third), dpre, (((0,), (0,)), ((), ())),
                preferred_element_type=jnp.float32,
            ) * (scale * LIFT)
            if s > 0:
                term = term + got[h].astype(jnp.float32)
            got[h] = around(term.astype(jnp.float16)) if s < NZ - 1 else term * (1.0 / LIFT)
    grads = jnp.concatenate(got, 0)
    return (grads[None], new_anchor, new_momentum)


def solution(mesh):
    placed = (
        P(("replica", "fsdp"), None),
        P(("replica", "fsdp"), None),
        P("replica", "fsdp", None),
        P("fsdp", None),
        P("fsdp", None),
        P(),
        P(),
    )
    return jax.shard_map(
        on_device,
        mesh=mesh,
        in_specs=placed,
        out_specs=(P("replica", "fsdp", None), P("fsdp", None), P("fsdp", None)),
        check_vma=False,
    )
```

```python
import math

import jax
import jax.numpy as jnp
from jax import lax
from jax.experimental import pallas as pl
from jax.experimental.pallas import tpu as pltpu
from jax.sharding import PartitionSpec as P

D = 12288
NFRAG = 4
REP = 16
FSDP = 16
NZ = 8
KEPT = NFRAG - 1

outer_mu = 0.9
outer_rate = 0.7
warm_steps = 8.0
mix_keep = 0.5
LIFT = 32.0

RING = [
    (r * FSDP + yh * NZ + z, r * FSDP + yh * NZ + (z + 1 - 2 * (r % 2)) % NZ)
    for r in range(REP)
    for yh in range(2)
    for z in range(NZ)
]
YLO = [(r, r ^ 8) for r in range(REP)]
CORE = [(r, r ^ 1) for r in range(REP)]
X1 = [(r, r ^ 2) for r in range(REP)]
X3 = [(r, r ^ 6) for r in range(REP)]
SWAP = [(f, (f + NZ) % FSDP) for f in range(FSDP)]

WHOLE = pl.BlockSpec(memory_space=pltpu.VMEM)
SCALARS = pl.BlockSpec(memory_space=pltpu.SMEM)
ANY = pl.BlockSpec(memory_space=pl.ANY)


def around(x):
    return lax.ppermute(x, ("replica", "fsdp"), RING)


def back(x):
    return lax.ppermute(x, ("replica", "fsdp"), [(b, a) for a, b in RING])


def across(x):
    return lax.ppermute(x, "fsdp", SWAP)


def after(x, *deps):
    def kernel(*refs):
        del refs

    return pl.pallas_call(
        kernel,
        out_shape=jax.ShapeDtypeStruct(x.shape, x.dtype),
        in_specs=[ANY] * (1 + len(deps)),
        out_specs=ANY,
        input_output_aliases={0: 0},
        cost_estimate=pl.CostEstimate(flops=0, bytes_accessed=0, transcendentals=0),
    )(x, *deps)


def split(tokens, cotangent, mine, *deps):
    toks, half = tokens.shape[0], tokens.shape[1] // 2
    more = cotangent.shape[1]

    def kernel(at_ref, tokens_ref, cot_ref, *rest):
        send_ref, own_ref, sems = rest[-3:]
        own = pl.multiple_of(at_ref[0] * half, 128)
        other = pl.multiple_of((1 - at_ref[0]) * half, 128)
        copies = [
            pltpu.make_async_copy(
                tokens_ref.at[:, pl.ds(other, half)], send_ref.at[:, pl.ds(0, half)], sems.at[0]
            ),
            pltpu.make_async_copy(cot_ref, send_ref.at[:, pl.ds(half, more)], sems.at[1]),
            pltpu.make_async_copy(tokens_ref.at[:, pl.ds(own, half)], own_ref, sems.at[2]),
        ]
        for copy in copies:
            copy.start()
        for copy in copies:
            copy.wait()

    return pl.pallas_call(
        kernel,
        out_shape=(
            jax.ShapeDtypeStruct((toks, half + more), tokens.dtype),
            jax.ShapeDtypeStruct((toks, half), tokens.dtype),
        ),
        in_specs=[SCALARS] + [ANY] * (2 + len(deps)),
        out_specs=(WHOLE, WHOLE),
        scratch_shapes=[pltpu.SemaphoreType.DMA((3,))],
        compiler_params=pltpu.CompilerParams(vmem_limit_bytes=10 * 2**20),
        cost_estimate=pl.CostEstimate(
            flops=0, bytes_accessed=4 * tokens.size, transcendentals=0
        ),
        name="split",
    )(mine.astype(jnp.int32).reshape(1), tokens, cotangent, *deps)


def product(x, at, shards):
    count = len(shards[0])
    flat = [w for shard in shards for w in shard]
    size, cols = flat[0].shape

    def kernel(at_ref, x_ref, *rest):
        shard_refs, (out_ref, held, sems) = rest[:-3], rest[-3:]
        copies = [
            pltpu.make_async_copy(
                w, held.at[n // count, pl.ds(n % count * size, size), :], sems.at[n]
            )
            for n, w in enumerate(shard_refs)
        ]
        for copy in copies:
            copy.start()
        total = None
        for n, copy in enumerate(copies):
            copy.wait()
            if n % count < count - 1:
                continue
            step = n // count
            start = pl.multiple_of(at_ref[step], 128)
            term = jnp.dot(
                x_ref[:, pl.ds(start, count * size)],
                held[step],
                preferred_element_type=jnp.float32,
            )
            total = term if total is None else total + term
        out_ref[...] = total

    return pl.pallas_call(
        kernel,
        out_shape=jax.ShapeDtypeStruct((x.shape[0], cols), jnp.float32),
        in_specs=[SCALARS, WHOLE] + [ANY] * len(flat),
        out_specs=WHOLE,
        scratch_shapes=[
            pltpu.VMEM((len(shards), count * size, cols), x.dtype),
            pltpu.SemaphoreType.DMA((len(flat),)),
        ],
        compiler_params=pltpu.CompilerParams(vmem_limit_bytes=12 * 2**20),
        cost_estimate=pl.CostEstimate(
            flops=2 * x.shape[0] * x.shape[1] * cols,
            bytes_accessed=x.size * 2 + x.shape[1] * cols * 2 + x.shape[0] * cols * 4,
            transcendentals=0,
        ),
        name="product",
    )(at, x, *flat)


MIX_AT = 3


def on_device(tokens, cotangent, local_weight, anchor, momentum, fragment, counter):
    width = anchor.shape[1]
    frag = fragment[0] % NFRAG
    eta = outer_rate * jnp.minimum(
        jnp.float32(1.0), (counter[0].astype(jnp.float32) + 1.0) / warm_steps
    )
    scale = 1.0 / math.sqrt(D)
    local = local_weight[0]
    rows, hidden = local.shape
    f = lax.axis_index("fsdp")
    yh, z = f // NZ, f % NZ
    step = 1 - 2 * (lax.axis_index("replica") % 2)
    half = D // 2
    toks = tokens.shape[0]

    def columns(x, k):
        return lax.dynamic_slice_in_dim(x, (frag + 1 + k) % NFRAG * width, width, 1)

    def kept(x):
        return jnp.concatenate([columns(x, k) for k in range(KEPT)], 1)

    part_rows = rows // 2
    w = kept(local)
    shards = [[w[:part_rows], w[part_rows:]]]
    for s in range(NZ - 1):
        shards.append([around(v) for v in shards[s]])

    def swapped(v, perm):
        return lax.ppermute(v, "replica", perm)

    core = lax.axis_index("replica") % 2
    frag_local = columns(local, KEPT)
    frag_sum = frag_local.astype(jnp.float32) + swapped(frag_local, YLO).astype(jnp.float32)
    low, high = frag_sum[:part_rows], frag_sum[part_rows:]
    part_sum = jnp.where(core == 0, low, high) + swapped(jnp.where(core == 0, high, low), CORE)
    near_sum = part_sum
    part_sum = part_sum + swapped(part_sum, X1)
    part_sum = part_sum + swapped(part_sum, X3)
    there = swapped(part_sum, CORE)
    frag_sum = jnp.where(
        core == 0,
        jnp.concatenate([part_sum, there], 0),
        jnp.concatenate([there, part_sum], 0),
    )
    delta = anchor - frag_sum / REP
    new_momentum = outer_mu * momentum + delta
    new_anchor = anchor - eta * (outer_mu * new_momentum + delta)
    mixed = (
        mix_keep * frag_local.astype(jnp.float32) + (1.0 - mix_keep) * new_anchor
    ).astype(jnp.bfloat16)

    mixed = after(mixed, *shards[MIX_AT])
    ups, downs = [mixed], [mixed]
    for s in range(NZ // 2):
        ups.append(around(ups[s]))
        if s < NZ // 2 - 1:
            downs.append(back(downs[s]))
    last = ups + downs[:0:-1]

    send, own = split(tokens, cotangent, yh, near_sum, *shards[1])
    moved = across(send)
    x = jnp.concatenate([own, moved[:, :half]], 0)
    cot = jnp.concatenate([cotangent, moved[:, half:]], 0)

    def features(s, row, size):
        return lax.dynamic_slice_in_dim(x, (z - step * s + 2 * NZ) % NZ * rows + row, size, 1)

    at = jnp.stack([(z - step * s + NZ) % NZ * rows for s in range(NZ)]).astype(jnp.int32)

    def backward(total, up):
        part = total * scale
        got = across(part.astype(jnp.float16)).astype(jnp.float32)
        pre = part + jnp.concatenate([got[toks:], got[:toks]], 0)
        _, pull = jax.vjp(jax.nn.gelu, pre)
        return pull(up.astype(jnp.float32))[0].astype(jnp.bfloat16)

    dpre = jnp.concatenate(
        [
            backward(product(x, at, shards), kept(cot)),
            backward(product(x, at, [[v] for v in last]), columns(cot, KEPT)),
        ],
        1,
    )
    dpre = jnp.concatenate(
        [
            lax.dynamic_slice_in_dim(dpre, (b - frag - 1 + 2 * NFRAG) % NFRAG * width, width, 1)
            for b in range(NFRAG)
        ],
        1,
    )

    third = rows // 3
    got = [None] * 3
    for s in range(NZ):
        for h in range(3):
            term = lax.dot_general(
                features(1 + s, h * third, third), dpre, (((0,), (0,)), ((), ())),
                preferred_element_type=jnp.float32,
            ) * (scale * LIFT)
            if s > 0:
                term = term + got[h].astype(jnp.float32)
            got[h] = around(term.astype(jnp.float16)) if s < NZ - 1 else term * (1.0 / LIFT)
    grads = jnp.concatenate(got, 0)
    return (grads[None], new_anchor, new_momentum)


def solution(mesh):
    placed = (
        P(("replica", "fsdp"), None),
        P(("replica", "fsdp"), None),
        P("replica", "fsdp", None),
        P("fsdp", None),
        P("fsdp", None),
        P(),
        P(),
    )
    return jax.shard_map(
        on_device,
        mesh=mesh,
        in_specs=placed,
        out_specs=(P("replica", "fsdp", None), P("fsdp", None), P("fsdp", None)),
        check_vma=False,
    )
```
